32 devices in a mesh: group: 2 (over y), tile: 4 (over z), head: 4 (over x, core).
Axes of the slice: x: 2, y: 2, z: 4, core: 2. Of those that a mesh axis runs over, the one named last changes fastest.
Arguments:
- latent: bfloat16 [32, 6, 32, 3072], P(('group', 'tile'), None, None, 'head'), parts along dimension 0, may hold values from -6 to 6
- text_tokens: bfloat16 [512, 3072], P('group'), parts along dimension 0, may hold values from -6 to 6
- mod_shift: float32 [3072], replicated, may hold values from -3 to 3
- mod_scale: float32 [3072], replicated, may hold values from -2.5 to 2.5
- mod_gate: float32 [3072], replicated, may hold values from 0.5 to 2
- project_in: bfloat16 [3072, 3, 3072], P(None, None, 'head')
- project_out: bfloat16 [3072, 3072], P('head'), may hold values from -0.109375 to 0.109375
- q_gain: float32 [128], replicated, may hold values from 0.7 to 7
- k_gain: float32 [128], replicated, may hold values from 0.7 to 7
- pattern: int32 [8, 4], P('tile'), may hold values from 0 to 5, as said below
- tile_rows: int32 [16], P('group'), parts along dimension 0, may hold values from 96 to 384, as said below
- text_mask: int32 [512], P('group'), parts along dimension 0, may hold values from 0 to 1, as said below
Outputs:
- update: bfloat16 [32, 6, 32, 3072], P(('group', 'head'), None, 'tile'), parts along dimension 0
- text_update: bfloat16 [512, 3072], P(('group', 'head')), parts along dimension 0
The draws below stay inside these ranges and needn't reach their ends.
There are 2 independent parts, one for each index of `group`. The reference program is written for one: setup_inputs(seed, part) draws one part's arguments, and reference() takes and returns one part's arrays. A program takes and returns all parts, laid end to end along the dimension named above; an argument that names none is the same for every part. Nothing has to cross between parts.
Inputs may be any that keep to these rules, and one draw needn't show every extreme that they name: `pattern`: entries of a row are distinct, the first is the query tile itself (s = 2 + its index in its band), and none names a band outside the grid. `tile_rows`: tiles of the last column band hold from 96 to 384 real tokens; every other tile holds 384. `text_mask`: the ones form a prefix of at least 32 positions.
All inputs are finite; a program needn't handle non-finite values.
Results may differ from the reference program's by a relative error of at most 0.015.
The reference program's roundings to bfloat16 on the way count: a program that leaves them out, or rounds other values in their place, can miss the bound.
Values may be sent and summed in bfloat16 or wider, within the bound.
A program may use at most 128 MiB of HBM per device.

```python
import math
import jax
import jax.numpy as jnp
from jax import lax

D = 3072
HEADS = 24
HD = 128
F = 16
H = 6
TF = 8
TH = 6
TW = 8
NWIN = 4
TEXT = 256
W = 32
N_HEAD = 4


def draw_project_in(key, part):
    base = jax.random.normal(jax.random.fold_in(key, 11), (D, 3, HEADS * HD), jnp.float32) / math.sqrt(D)
    return base.astype(jnp.bfloat16)


def draw_q_gain(key, part):
    return jax.random.uniform(jax.random.fold_in(key, 21), (HD,), jnp.float32, 0.7, 1.6)


def draw_k_gain(key, part):
    return jax.random.uniform(jax.random.fold_in(key, 22), (HD,), jnp.float32, 0.7, 1.6)


def draw_pattern(key, part):
    band_count = W // TW
    per_device = F // TF * (H // TH)
    tile_total = per_device * band_count
    tile_ids = jnp.arange(tile_total, dtype=jnp.int32)
    owners = tile_ids // per_device
    local_ids = tile_ids % per_device
    slot_ids = jnp.arange(3 * per_device, dtype=jnp.int32)
    targets = owners[:, None] + slot_ids[None, :] // per_device - 1
    inside = (targets >= 0) & (targets < band_count)
    itself = slot_ids[None, :] == (per_device + local_ids)[:, None]
    ranking = jax.random.randint(jax.random.fold_in(key, 31), (tile_total, 3 * per_device), 0, 1 << 20) * 64 + slot_ids[None, :]
    ranking = jnp.where(inside & jnp.logical_not(itself), ranking, -1)
    picked_scores, picked = lax.top_k(ranking, NWIN - 1)
    return jnp.concatenate([(per_device + local_ids)[:, None], picked.astype(jnp.int32)], axis=1).astype(jnp.int32)


def draw_tile_rows(key, part):
    band_count = W // TW
    per_device = F // TF * (H // TH)
    tile_size = TF * TH * TW
    tile_ids = jnp.arange(per_device * band_count, dtype=jnp.int32)
    shorter = jax.random.randint(jax.random.fold_in(key, 41), (per_device * band_count,), tile_size // 4, tile_size + 1)
    return jnp.where(tile_ids // per_device == band_count - 1, shorter, tile_size).astype(jnp.int32)


def draw_text_mask(key, part):
    prompt_length = jax.random.randint(jax.random.fold_in(key, 51), (), TEXT // 8, TEXT + 1)
    return (jnp.arange(TEXT, dtype=jnp.int32) < prompt_length).astype(jnp.int32)


def block_levels(stream_key, dims, split, low, largest):
    gain = 1.0
    for dim, parts in split:
        draws = jax.random.uniform(jax.random.fold_in(jax.random.fold_in(stream_key, 6), dim), (parts,), jnp.float32, low / len(split), largest / len(split))
        gain = gain * jnp.repeat(jnp.exp(draws), dims[dim] // parts).reshape((-1,) + (1,) * (len(dims) - 1 - dim))
    return gain


def gaussian(stream_key, shape, width, bound, split=(), kind=jnp.bfloat16):
    level = block_levels(stream_key, shape, split, -0.22, 0.18) if split else 1.0
    result = jax.random.normal(stream_key, shape, jnp.float32) * width * level
    return jnp.minimum(jnp.maximum(result, -bound), bound).astype(kind)


def setup_inputs(seed: int = 0, part: int = 0) -> dict:
    seeds = jax.random.split(jax.random.key(seed), 13)
    own_keys = jax.random.split(jax.random.fold_in(seeds[12], part), 13)
    latent = gaussian(own_keys[0], (F, H, W, D), 1.0, 6.0, ((0, 4), (3, 4)))
    text_tokens = gaussian(own_keys[1], (TEXT, D), 1.0, 6.0)
    mod_shift = gaussian(seeds[2], (D,), 0.5, 3.0, (), jnp.float32)
    mod_scale = gaussian(seeds[3], (D,), 0.5, 2.5, (), jnp.float32)
    mod_gate = jnp.clip(jax.random.uniform(seeds[4], (D,), jnp.float32, 0.5, 2.0), 0.5, 2.0)
    project_in = draw_project_in(jax.random.fold_in(seeds[12], 71), part)
    project_out = gaussian(seeds[6], (HEADS * HD, D), (HEADS * HD) ** -0.5, 0.109375, ((0, 4),))
    q_gain = draw_q_gain(jax.random.fold_in(seeds[12], 71), part)
    k_gain = draw_k_gain(jax.random.fold_in(seeds[12], 71), part)
    pattern = draw_pattern(jax.random.fold_in(seeds[12], 71), part)
    tile_rows = draw_tile_rows(jax.random.fold_in(jax.random.fold_in(seeds[12], part), 71), part)
    text_mask = draw_text_mask(jax.random.fold_in(jax.random.fold_in(seeds[12], part), 71), part)
    return dict(latent=latent, text_tokens=text_tokens, mod_shift=mod_shift, mod_scale=mod_scale, mod_gate=mod_gate, project_in=project_in, project_out=project_out, q_gain=q_gain, k_gain=k_gain, pattern=pattern, tile_rows=tile_rows, text_mask=text_mask)


EPSILON = 1e-06

def modulate(values, mod_shift, mod_scale):
    widened = values.astype(jnp.float32)
    center = lax.optimization_barrier(jnp.mean(widened, axis=-1, keepdims=True))
    offset = widened - center
    variance = lax.optimization_barrier(jnp.mean(offset * offset, axis=-1, keepdims=True))
    return (offset * lax.rsqrt(variance + EPSILON) * (1.0 + mod_scale) + mod_shift).astype(jnp.bfloat16)

def rms_gain(values, gains):
    square = lax.optimization_barrier(jnp.mean(values * values, axis=-1, keepdims=True))
    return (values * lax.rsqrt(square + EPSILON) * gains).astype(jnp.bfloat16)

def attend(queries, key_rows, value_rows, usable):
    scores = jnp.einsum('qhd,khd->hqk', queries.astype(jnp.float32), key_rows.astype(jnp.float32), precision=lax.Precision.HIGHEST) / math.sqrt(HD)
    scores = jnp.where(usable[None, None, :], scores, -jnp.inf)
    highest = lax.optimization_barrier(jnp.max(scores, axis=-1, keepdims=True))
    weights = jnp.exp(scores - highest)
    sums_row = lax.optimization_barrier(jnp.sum(weights, axis=-1))
    rounded = lax.optimization_barrier(weights.astype(jnp.bfloat16)).astype(jnp.float32)
    blended = jnp.einsum('hqk,khd->qhd', rounded, value_rows.astype(jnp.float32), precision=lax.Precision.HIGHEST)
    return (blended / jnp.transpose(sums_row)[:, :, None]).astype(jnp.bfloat16)

def reference(latent, text_tokens, mod_shift, mod_scale, mod_gate, project_in, project_out, q_gain, k_gain, pattern, tile_rows, text_mask):
    time_tiles = F // TF
    row_tiles = H // TH
    band_count = W // TW
    per_device = time_tiles * row_tiles
    tile_size = TF * TH * TW
    tile_total = per_device * band_count
    flat_in = project_in.reshape(D, 3 * HEADS * HD)

    def prepare(token_rows):
        product = jnp.dot(modulate(token_rows, mod_shift, mod_scale), flat_in, preferred_element_type=jnp.float32)
        product = product.reshape(token_rows.shape[0], 3, HEADS, HD)
        return (rms_gain(product[:, 0], q_gain), rms_gain(product[:, 1], k_gain), product[:, 2].astype(jnp.bfloat16))
    arranged = latent.reshape(time_tiles, TF, row_tiles, TH, band_count, TW, D)
    arranged = jnp.transpose(arranged, (4, 0, 2, 1, 3, 5, 6)).reshape(tile_total, tile_size, D)
    tile_queries, tile_keys, tile_values = lax.map(prepare, arranged)
    text_queries, text_keys, text_values = prepare(text_tokens)
    positions = jnp.arange(tile_size, dtype=jnp.int32)
    tile_usable = positions[None, :] < tile_rows[:, None]
    text_usable = text_mask == 1
    owners = jnp.arange(tile_total, dtype=jnp.int32) // per_device
    key_tiles = ((owners[:, None] + pattern // per_device - 1) * per_device + pattern % per_device).astype(jnp.int32)

    def latent_tile(tile_id):
        chosen = key_tiles[tile_id]
        key_rows = jnp.concatenate([tile_keys[chosen].reshape(-1, HEADS, HD), text_keys], 0)
        value_rows = jnp.concatenate([tile_values[chosen].reshape(-1, HEADS, HD), text_values], 0)
        usable = jnp.concatenate([tile_usable[chosen].reshape(-1), text_usable], 0)
        return attend(tile_queries[tile_id], key_rows, value_rows, usable)
    latent_out = lax.map(latent_tile, jnp.arange(tile_total, dtype=jnp.int32))
    latent_out = jnp.where(tile_usable[:, :, None, None], latent_out, jnp.zeros_like(latent_out))
    every_keys = jnp.concatenate([tile_keys.reshape(-1, HEADS, HD), text_keys], 0)
    every_values = jnp.concatenate([tile_values.reshape(-1, HEADS, HD), text_values], 0)
    every_usable = jnp.concatenate([tile_usable.reshape(-1), text_usable], 0)

    def text_head(head_id):

        def select_head(source):
            return lax.dynamic_slice_in_dim(source, head_id, 1, 1)
        return attend(select_head(text_queries), select_head(every_keys), select_head(every_values), every_usable)[:, 0]
    text_out = jnp.transpose(lax.map(text_head, jnp.arange(HEADS, dtype=jnp.int32)), (1, 0, 2))
    group_width = HEADS * HD // N_HEAD

    def out_project(attention_rows):
        accum = jnp.zeros((attention_rows.shape[0], D), jnp.float32)
        for group_id in range(N_HEAD):
            lower = group_id * group_width
            partial_term = jnp.dot(attention_rows[:, lower:lower + group_width], project_out[lower:lower + group_width], preferred_element_type=jnp.float32)
            accum = accum + lax.optimization_barrier(partial_term.astype(jnp.bfloat16)).astype(jnp.float32)
        return (accum * mod_gate).astype(jnp.bfloat16)
    latent_rows = out_project(latent_out.reshape(-1, HEADS * HD))
    update = latent_rows.reshape(band_count, time_tiles, row_tiles, TF, TH, TW, D)
    update = jnp.transpose(update, (1, 3, 2, 4, 0, 5, 6)).reshape(F, H, W, D)
    text_update = out_project(text_out.reshape(TEXT, HEADS * HD))
    return (update, text_update)
```

```python
import functools
import math

import jax
import jax.numpy as jnp
from jax import lax
from jax.experimental import pallas as pl
from jax.experimental.pallas import tpu as pltpu
from jax.sharding import PartitionSpec as P

D = 3072
HD = 128
F = 16
H = 6
TF = 8
TH = 6
TW = 8
TEXT = 256


EPSILON = 1e-06


def modulate(values, mod_shift, mod_scale):
    widened = values.astype(jnp.float32)
    center = jnp.mean(widened, axis=-1, keepdims=True)
    offset = widened - center
    variance = jnp.mean(offset * offset, axis=-1, keepdims=True)
    return (offset * lax.rsqrt(variance + EPSILON) * (1.0 + mod_scale) + mod_shift).astype(
        jnp.bfloat16
    )


def rms_gain(values, gains):
    square = jnp.mean(values * values, axis=-1, keepdims=True)
    return (values * lax.rsqrt(square + EPSILON) * gains).astype(jnp.bfloat16)


def prepare(normed, project_in, q_gain, k_gain):
    product = jnp.einsum("td,dcn->tcn", normed, project_in, preferred_element_type=jnp.float32)
    count, _, width = product.shape

    def heads_of(index):
        return product[:, index].reshape(count, width // HD, HD)

    query_part = rms_gain(heads_of(0), q_gain).reshape(count, width)
    key_part = rms_gain(heads_of(1), k_gain).reshape(count, width)
    return (query_part, key_part, product[:, 2].astype(jnp.bfloat16))


SCALE = math.log2(math.e) / math.sqrt(HD)
MASKED = -1e30


def softmax_blend(queries, chunks):
    logits = []
    for keys, _, bias in chunks:
        raw = lax.dot_general(
            queries, keys, (((1,), (1,)), ((), ())), preferred_element_type=jnp.float32
        )
        logits.append(raw * SCALE + bias)
    highest = jnp.max(logits[0], axis=-1, keepdims=True)
    for part in logits[1:]:
        highest = jnp.maximum(highest, jnp.max(part, axis=-1, keepdims=True))
    sums = None
    blended = None
    for part, (_, values, _) in zip(logits, chunks):
        weights = jnp.exp2(part - highest)
        row = jnp.sum(weights, axis=-1, keepdims=True)
        term = jnp.dot(
            weights.astype(jnp.bfloat16), values, preferred_element_type=jnp.float32
        )
        sums = row if sums is None else sums + row
        blended = term if blended is None else blended + term
    return highest, sums, blended


def latent_kernel(per_device, tile_size, slots, rows_ref, q_ref, own_k, own_v, low_k, low_v,
                  high_k, high_v, text_k, text_v, bias_ref, text_bias, out_ref, keys, values):
    for band, (k_ref, v_ref) in enumerate(((low_k, low_v), (own_k, own_v), (high_k, high_v))):
        for local in range(per_device):
            rows = pl.ds(local * tile_size, tile_size)
            keys[band * per_device + local] = k_ref[rows, :]
            values[band * per_device + local] = v_ref[rows, :]
    for local in range(per_device):
        rows = pl.ds(local * tile_size, tile_size)
        chunks = []
        for s in range(slots):
            slot = rows_ref[1 + local, s]
            chunks.append((keys[slot], values[slot], bias_ref[local, s]))
        chunks.append((text_k[...], text_v[...], text_bias[...]))
        _, sums, blended = softmax_blend(q_ref[rows, :], chunks)
        place = lax.broadcasted_iota(jnp.int32, (tile_size, HD), 0)
        out_ref[rows, :] = jnp.where(
            place < rows_ref[0, local], blended / sums, 0.0
        ).astype(jnp.bfloat16)


def text_kernel(q_ref, own_k, own_v, text_k, text_v, own_bias, text_bias, out_ref, level_ref):
    chunks = (
        (own_k[...], own_v[...], own_bias[...]),
        (text_k[...], text_v[...], text_bias[...]),
    )
    highest, sums, blended = softmax_blend(q_ref[...], chunks)
    out_ref[...] = (blended / sums).astype(jnp.bfloat16)
    level_ref[...] = jnp.broadcast_to(highest + jnp.log2(sums), level_ref.shape)


def column(rows):
    return pl.BlockSpec((rows, HD), lambda head, *_: (0, head))


def fixed(shape):
    return pl.BlockSpec(shape, lambda head, *_: (0,) * len(shape))


def shards(
    latent,
    text_tokens,
    mod_shift,
    mod_scale,
    mod_gate,
    project_in,
    project_out,
    q_gain,
    k_gain,
    pattern,
    tile_rows,
    text_mask,
):
    head_count = lax.axis_size("head")
    band_count = lax.axis_size("tile")
    band_index = lax.axis_index("tile")
    moved = lax.all_to_all(latent, "tile", split_axis=2, concat_axis=0, tiled=True)
    column_whole = lax.all_gather(moved, "head", axis=3, tiled=True)
    normed = modulate(column_whole, mod_shift, mod_scale).reshape(-1, D)
    own_q, own_k, own_v = prepare(normed, project_in, q_gain, k_gain)
    text_q, text_k, text_v = prepare(
        modulate(text_tokens, mod_shift, mod_scale), project_in, q_gain, k_gain
    )
    count, width = own_q.shape
    local_heads = width // HD
    per_device = F // TF * (H // TH)
    tile_size = TF * TH * TW
    slots = pattern.shape[1]
    forward = [(i, i + 1) for i in range(band_count - 1)]
    backward = [(target, source) for source, target in forward]
    low_k, low_v = (lax.ppermute(part, "tile", forward) for part in (own_k, own_v))
    high_k, high_v = (lax.ppermute(part, "tile", backward) for part in (own_k, own_v))

    positions = jnp.arange(tile_size, dtype=jnp.int32)
    text_usable = text_mask == 1
    slot_band = band_index + pattern // per_device - 1
    picked_rows = tile_rows[
        jnp.clip(slot_band, 0, band_count - 1) * per_device + pattern % per_device
    ]
    bias = jnp.where(positions < picked_rows[..., None], 0.0, MASKED).astype(jnp.float32)
    bias = bias.reshape(per_device, slots, 1, tile_size)
    text_bias = jnp.where(text_usable, 0.0, MASKED).astype(jnp.float32)[None]
    own_rows = lax.dynamic_slice_in_dim(tile_rows, band_index * per_device, per_device, 0)
    own_bias = jnp.where(positions[None] < own_rows[:, None], 0.0, MASKED)
    own_bias = own_bias.astype(jnp.float32).reshape(1, count)
    once_bias = jnp.where(band_index == 0, text_bias, MASKED)

    text_part, levels = pl.pallas_call(
        text_kernel,
        grid=(local_heads,),
        in_specs=[
            column(TEXT), column(count), column(count), column(TEXT), column(TEXT),
            fixed((1, count)), fixed((1, TEXT)),
        ],
        out_specs=[column(TEXT), column(TEXT)],
        out_shape=[
            jax.ShapeDtypeStruct((TEXT, width), jnp.bfloat16),
            jax.ShapeDtypeStruct((TEXT, width), jnp.float32),
        ],
        compiler_params=pltpu.CompilerParams(vmem_limit_bytes=48 << 20),
        cost_estimate=pl.CostEstimate(
            flops=4 * TEXT * (count + TEXT) * width, bytes_accessed=6 << 20, transcendentals=0
        ),
        name="text_attention",
    )(text_q, own_k, own_v, text_k, text_v, own_bias, once_bias)
    level = levels.reshape(TEXT, local_heads, HD)[:, :, 0]
    distance = 1
    while distance < band_count:
        pairs = [(i, i ^ distance) for i in range(band_count)]
        other_part = lax.ppermute(text_part, "tile", pairs)
        other_level = lax.ppermute(level, "tile", pairs)
        peak = jnp.maximum(level, other_level)
        mine, theirs = jnp.exp2(level - peak), jnp.exp2(other_level - peak)
        total = mine + theirs

        def widen(share):
            return jnp.repeat(share, HD, axis=1)

        text_part = (
            text_part.astype(jnp.float32) * widen(mine / total)
            + other_part.astype(jnp.float32) * widen(theirs / total)
        ).astype(jnp.bfloat16)
        level = peak + jnp.log2(total)
        distance *= 2

    filler = jnp.zeros((1, slots - per_device), jnp.int32)
    numbers = jnp.concatenate(
        [jnp.concatenate([own_rows[None].astype(jnp.int32), filler], 1), pattern], 0
    )
    latent_out = pl.pallas_call(
        functools.partial(latent_kernel, per_device, tile_size, slots),
        grid_spec=pltpu.PrefetchScalarGridSpec(
            num_scalar_prefetch=1,
            grid=(local_heads,),
            in_specs=[column(count)] * 7 + [column(TEXT)] * 2
            + [fixed((per_device, slots, 1, tile_size)), fixed((1, TEXT))],
            out_specs=column(count),
            scratch_shapes=[pltpu.VMEM((3 * per_device, tile_size, HD), jnp.bfloat16)] * 2,
        ),
        out_shape=jax.ShapeDtypeStruct((count, width), jnp.bfloat16),
        compiler_params=pltpu.CompilerParams(vmem_limit_bytes=48 << 20),
        cost_estimate=pl.CostEstimate(
            flops=4 * count * (slots * tile_size + TEXT) * width,
            bytes_accessed=10 << 20, transcendentals=0,
        ),
        name="latent_attention",
    )(numbers, own_q, own_k, own_v, low_k, low_v, high_k, high_v, text_k, text_v, bias, text_bias)

    latent_columns = latent_out.reshape(head_count, -1, width)
    text_blocks = text_part.reshape(head_count, -1, width)
    latent_share = latent_columns.shape[1]
    joined = jnp.concatenate([latent_columns, text_blocks], 1).reshape(-1, width)
    summed_rows = lax.psum_scatter(
        jnp.dot(joined, project_out, preferred_element_type=jnp.float32).astype(jnp.bfloat16),
        "head",
        scatter_dimension=0,
        tiled=True,
    ).astype(jnp.float32)
    update = (
        (summed_rows[:latent_share] * mod_gate)
        .astype(jnp.bfloat16)
        .reshape(F // head_count, H, TW, D)
    )
    text_update = (summed_rows[latent_share:] * mod_gate).astype(jnp.bfloat16)
    return (update, text_update)


def solution(mesh):
    placed = (
        P(("group", "tile"), None, None, "head"),
        P("group", None),
        P(),
        P(),
        P(),
        P(None, None, "head"),
        P("head", None),
        P(),
        P(),
        P("tile", None),
        P("group"),
        P("group"),
    )
    return jax.shard_map(
        shards,
        mesh=mesh,
        in_specs=placed,
        out_specs=(P(("group", "head"), None, "tile", None), P(("group", "head"), None)),
        check_vma=False,
    )
```

```python
import functools
import math

import jax
import jax.numpy as jnp
from jax import lax
from jax.experimental import pallas as pl
from jax.experimental.pallas import tpu as pltpu
from jax.sharding import PartitionSpec as P

D = 3072
HD = 128
F = 16
H = 6
TF = 8
TH = 6
TW = 8
TEXT = 256


EPSILON = 1e-06


def modulate(values, mod_shift, mod_scale):
    widened = values.astype(jnp.float32)
    center = jnp.mean(widened, axis=-1, keepdims=True)
    offset = widened - center
    variance = jnp.mean(offset * offset, axis=-1, keepdims=True)
    return (offset * lax.rsqrt(variance + EPSILON) * (1.0 + mod_scale) + mod_shift).astype(
        jnp.bfloat16
    )


def rms_gain(values, gains):
    square = jnp.mean(values * values, axis=-1, keepdims=True)
    return (values * lax.rsqrt(square + EPSILON) * gains).astype(jnp.bfloat16)


def norm_kernel(product_ref, q_gain, k_gain, q_ref, k_ref, v_ref):
    q_ref[...] = rms_gain(product_ref[0], q_gain[...])
    k_ref[...] = rms_gain(product_ref[1], k_gain[...])
    v_ref[...] = product_ref[2].astype(jnp.bfloat16)


def prepare(normed, project_in, q_gain, k_gain):
    product = jnp.einsum("td,dcn->ctn", normed, project_in, preferred_element_type=jnp.float32)
    _, count, width = product.shape
    return pl.pallas_call(
        norm_kernel,
        grid=(width // HD,),
        in_specs=[
            pl.BlockSpec((3, count, HD), lambda head: (0, 0, head)),
            fixed((1, HD)),
            fixed((1, HD)),
        ],
        out_specs=[column(count)] * 3,
        out_shape=[jax.ShapeDtypeStruct((count, width), jnp.bfloat16)] * 3,
        compiler_params=pltpu.CompilerParams(vmem_limit_bytes=32 << 20),
        cost_estimate=pl.CostEstimate(
            flops=8 * count * width, bytes_accessed=18 * count * width, transcendentals=0
        ),
        name="head_norm",
    )(product, q_gain[None], k_gain[None])


SCALE = math.log2(math.e) / math.sqrt(HD)
MASKED = -1e30


def softmax_blend(queries, chunks):
    logits = []
    for keys, _, bias in chunks:
        raw = lax.dot_general(
            queries, keys, (((1,), (1,)), ((), ())), preferred_element_type=jnp.float32
        )
        logits.append(raw * SCALE + bias)
    highest = jnp.max(logits[0], axis=-1, keepdims=True)
    for part in logits[1:]:
        highest = jnp.maximum(highest, jnp.max(part, axis=-1, keepdims=True))
    sums = None
    blended = None
    for part, (_, values, _) in zip(logits, chunks):
        weights = jnp.exp2(part - highest)
        row = jnp.sum(weights, axis=-1, keepdims=True)
        term = jnp.dot(
            weights.astype(jnp.bfloat16), values, preferred_element_type=jnp.float32
        )
        sums = row if sums is None else sums + row
        blended = term if blended is None else blended + term
    return highest, sums, blended


def latent_kernel(per_device, tile_size, slots, rows_ref, q_ref, own_k, own_v, low_k, low_v,
                  high_k, high_v, text_k, text_v, bias_ref, text_bias, out_ref, keys, values):
    for band, (k_ref, v_ref) in enumerate(((low_k, low_v), (own_k, own_v), (high_k, high_v))):
        for local in range(per_device):
            rows = pl.ds(local * tile_size, tile_size)
            keys[band * per_device + local] = k_ref[rows, :]
            values[band * per_device + local] = v_ref[rows, :]
    for local in range(per_device):
        rows = pl.ds(local * tile_size, tile_size)
        chunks = []
        for s in range(slots):
            slot = rows_ref[1 + local, s]
            chunks.append((keys[slot], values[slot], bias_ref[local, s]))
        chunks.append((text_k[...], text_v[...], text_bias[...]))
        _, sums, blended = softmax_blend(q_ref[rows, :], chunks)
        place = lax.broadcasted_iota(jnp.int32, (tile_size, HD), 0)
        out_ref[rows, :] = jnp.where(
            place < rows_ref[0, local], blended / sums, 0.0
        ).astype(jnp.bfloat16)


def text_kernel(q_ref, own_k, own_v, text_k, text_v, own_bias, text_bias, out_ref, level_ref):
    chunks = (
        (own_k[...], own_v[...], own_bias[...]),
        (text_k[...], text_v[...], text_bias[...]),
    )
    highest, sums, blended = softmax_blend(q_ref[...], chunks)
    out_ref[...] = (blended / sums).astype(jnp.bfloat16)
    level_ref[...] = jnp.broadcast_to(highest + jnp.log2(sums), level_ref.shape)


def column(rows):
    return pl.BlockSpec((rows, HD), lambda head, *_: (0, head))


def fixed(shape):
    return pl.BlockSpec(shape, lambda head, *_: (0,) * len(shape))


def shards(
    latent,
    text_tokens,
    mod_shift,
    mod_scale,
    mod_gate,
    project_in,
    project_out,
    q_gain,
    k_gain,
    pattern,
    tile_rows,
    text_mask,
):
    head_count = lax.axis_size("head")
    band_count = lax.axis_size("tile")
    band_index = lax.axis_index("tile")
    moved = lax.all_to_all(latent, "tile", split_axis=2, concat_axis=0, tiled=True)
    column_whole = lax.all_gather(moved, "head", axis=3, tiled=True)
    normed = modulate(column_whole, mod_shift, mod_scale).reshape(-1, D)
    own_q, own_k, own_v = prepare(normed, project_in, q_gain, k_gain)
    text_q, text_k, text_v = prepare(
        modulate(text_tokens, mod_shift, mod_scale), project_in, q_gain, k_gain
    )
    count, width = own_q.shape
    local_heads = width // HD
    per_device = F // TF * (H // TH)
    tile_size = TF * TH * TW
    slots = pattern.shape[1]
    forward = [(i, i + 1) for i in range(band_count - 1)]
    backward = [(target, source) for source, target in forward]
    low_k, low_v = (lax.ppermute(part, "tile", forward) for part in (own_k, own_v))
    high_k, high_v = (lax.ppermute(part, "tile", backward) for part in (own_k, own_v))

    positions = jnp.arange(tile_size, dtype=jnp.int32)
    text_usable = text_mask == 1
    slot_band = band_index + pattern // per_device - 1
    picked_rows = tile_rows[
        jnp.clip(slot_band, 0, band_count - 1) * per_device + pattern % per_device
    ]
    bias = jnp.where(positions < picked_rows[..., None], 0.0, MASKED).astype(jnp.float32)
    bias = bias.reshape(per_device, slots, 1, tile_size)
    text_bias = jnp.where(text_usable, 0.0, MASKED).astype(jnp.float32)[None]
    own_rows = lax.dynamic_slice_in_dim(tile_rows, band_index * per_device, per_device, 0)
    own_bias = jnp.where(positions[None] < own_rows[:, None], 0.0, MASKED)
    own_bias = own_bias.astype(jnp.float32).reshape(1, count)
    once_bias = jnp.where(band_index == 0, text_bias, MASKED)

    text_part, levels = pl.pallas_call(
        text_kernel,
        grid=(local_heads,),
        in_specs=[
            column(TEXT), column(count), column(count), column(TEXT), column(TEXT),
            fixed((1, count)), fixed((1, TEXT)),
        ],
        out_specs=[column(TEXT), column(TEXT)],
        out_shape=[
            jax.ShapeDtypeStruct((TEXT, width), jnp.bfloat16),
            jax.ShapeDtypeStruct((TEXT, width), jnp.float32),
        ],
        compiler_params=pltpu.CompilerParams(vmem_limit_bytes=48 << 20),
        cost_estimate=pl.CostEstimate(
            flops=4 * TEXT * (count + TEXT) * width, bytes_accessed=6 << 20, transcendentals=0
        ),
        name="text_attention",
    )(text_q, own_k, own_v, text_k, text_v, own_bias, once_bias)
    level = levels.reshape(TEXT, local_heads, HD)[:, :, 0]
    distance = 1
    while distance < band_count:
        pairs = [(i, i ^ distance) for i in range(band_count)]
        other_part = lax.ppermute(text_part, "tile", pairs)
        other_level = lax.ppermute(level, "tile", pairs)
        peak = jnp.maximum(level, other_level)
        mine, theirs = jnp.exp2(level - peak), jnp.exp2(other_level - peak)
        total = mine + theirs

        def widen(share):
            return jnp.repeat(share, HD, axis=1)

        text_part = (
            text_part.astype(jnp.float32) * widen(mine / total)
            + other_part.astype(jnp.float32) * widen(theirs / total)
        ).astype(jnp.bfloat16)
        level = peak + jnp.log2(total)
        distance *= 2

    filler = jnp.zeros((1, slots - per_device), jnp.int32)
    numbers = jnp.concatenate(
        [jnp.concatenate([own_rows[None].astype(jnp.int32), filler], 1), pattern], 0
    )
    latent_out = pl.pallas_call(
        functools.partial(latent_kernel, per_device, tile_size, slots),
        grid_spec=pltpu.PrefetchScalarGridSpec(
            num_scalar_prefetch=1,
            grid=(local_heads,),
            in_specs=[column(count)] * 7 + [column(TEXT)] * 2
            + [fixed((per_device, slots, 1, tile_size)), fixed((1, TEXT))],
            out_specs=column(count),
            scratch_shapes=[pltpu.VMEM((3 * per_device, tile_size, HD), jnp.bfloat16)] * 2,
        ),
        out_shape=jax.ShapeDtypeStruct((count, width), jnp.bfloat16),
        compiler_params=pltpu.CompilerParams(vmem_limit_bytes=48 << 20),
        cost_estimate=pl.CostEstimate(
            flops=4 * count * (slots * tile_size + TEXT) * width,
            bytes_accessed=10 << 20, transcendentals=0,
        ),
        name="latent_attention",
    )(numbers, own_q, own_k, own_v, low_k, low_v, high_k, high_v, text_k, text_v, bias, text_bias)

    latent_columns = latent_out.reshape(head_count, -1, width)
    text_blocks = text_part.reshape(head_count, -1, width)
    latent_share = latent_columns.shape[1]
    joined = jnp.concatenate([latent_columns, text_blocks], 1).reshape(-1, width)
    summed_rows = lax.psum_scatter(
        jnp.dot(joined, project_out, preferred_element_type=jnp.float32).astype(jnp.bfloat16),
        "head",
        scatter_dimension=0,
        tiled=True,
    ).astype(jnp.float32)
    update = (
        (summed_rows[:latent_share] * mod_gate)
        .astype(jnp.bfloat16)
        .reshape(F // head_count, H, TW, D)
    )
    text_update = (summed_rows[latent_share:] * mod_gate).astype(jnp.bfloat16)
    return (update, text_update)


def solution(mesh):
    placed = (
        P(("group", "tile"), None, None, "head"),
        P("group", None),
        P(),
        P(),
        P(),
        P(None, None, "head"),
        P("head", None),
        P(),
        P(),
        P("tile", None),
        P("group"),
        P("group"),
    )
    return jax.shard_map(
        shards,
        mesh=mesh,
        in_specs=placed,
        out_specs=(P(("group", "head"), None, "tile", None), P(("group", "head"), None)),
        check_vma=False,
    )
```

```python
import functools
import math

import jax
import jax.numpy as jnp
from jax import lax
from jax.experimental import pallas as pl
from jax.experimental.pallas import tpu as pltpu
from jax.sharding import PartitionSpec as P

D = 3072
HD = 128
F = 16
H = 6
TF = 8
TH = 6
TW = 8
TEXT = 256


EPSILON = 1e-06


def modulate(values, mod_shift, mod_scale):
    widened = values.astype(jnp.float32)
    center = jnp.mean(widened, axis=-1, keepdims=True)
    offset = widened - center
    variance = jnp.mean(offset * offset, axis=-1, keepdims=True)
    return (offset * lax.rsqrt(variance + EPSILON) * (1.0 + mod_scale) + mod_shift).astype(
        jnp.bfloat16
    )


def rms_gain(values, gains):
    square = jnp.mean(values * values, axis=-1, keepdims=True)
    return (values * lax.rsqrt(square + EPSILON) * gains).astype(jnp.bfloat16)


def norm_kernel(product_ref, q_gain, k_gain, q_ref, k_ref, v_ref):
    q_ref[...] = rms_gain(product_ref[0], q_gain[...])
    k_ref[...] = rms_gain(product_ref[1], k_gain[...])
    v_ref[...] = product_ref[2].astype(jnp.bfloat16)


def prepare(normed, project_in, q_gain, k_gain):
    product = jnp.einsum("td,dcn->ctn", normed, project_in, preferred_element_type=jnp.float32)
    _, count, width = product.shape
    return pl.pallas_call(
        norm_kernel,
        grid=(width // HD,),
        in_specs=[
            pl.BlockSpec((3, count, HD), lambda head: (0, 0, head)),
            fixed((1, HD)),
            fixed((1, HD)),
        ],
        out_specs=[column(count)] * 3,
        out_shape=[jax.ShapeDtypeStruct((count, width), jnp.bfloat16)] * 3,
        compiler_params=pltpu.CompilerParams(vmem_limit_bytes=32 << 20),
        cost_estimate=pl.CostEstimate(
            flops=8 * count * width, bytes_accessed=18 * count * width, transcendentals=0
        ),
        name="head_norm",
    )(product, q_gain[None], k_gain[None])


SCALE = math.log2(math.e) / math.sqrt(HD)
MASKED = -1e30


def softmax_blend(queries, chunks):
    logits = []
    for keys, _, bias in chunks:
        raw = lax.dot_general(
            queries, keys, (((1,), (1,)), ((), ())), preferred_element_type=jnp.float32
        )
        logits.append(raw * SCALE + bias)
    highest = jnp.max(logits[0], axis=-1, keepdims=True)
    for part in logits[1:]:
        highest = jnp.maximum(highest, jnp.max(part, axis=-1, keepdims=True))
    sums = None
    blended = None
    for part, (_, values, _) in zip(logits, chunks):
        weights = jnp.exp2(part - highest)
        row = jnp.sum(weights, axis=-1, keepdims=True)
        term = jnp.dot(
            weights.astype(jnp.bfloat16), values, preferred_element_type=jnp.float32
        )
        sums = row if sums is None else sums + row
        blended = term if blended is None else blended + term
    return highest, sums, blended


def latent_kernel(per_device, tile_size, slots, rows_ref, q_ref, own_k, own_v, low_k, low_v,
                  high_k, high_v, text_k, text_v, bias_ref, text_bias, out_ref, keys, values):
    for band, (k_ref, v_ref) in enumerate(((low_k, low_v), (own_k, own_v), (high_k, high_v))):
        for local in range(per_device):
            rows = pl.ds(local * tile_size, tile_size)
            keys[band * per_device + local] = k_ref[rows, :]
            values[band * per_device + local] = v_ref[rows, :]
    for local in range(per_device):
        rows = pl.ds(local * tile_size, tile_size)
        chunks = []
        for s in range(slots):
            slot = rows_ref[1 + local, s]
            chunks.append((keys[slot], values[slot], bias_ref[local, s]))
        chunks.append((text_k[...], text_v[...], text_bias[...]))
        _, sums, blended = softmax_blend(q_ref[rows, :], chunks)
        place = lax.broadcasted_iota(jnp.int32, (tile_size, HD), 0)
        out_ref[rows, :] = jnp.where(
            place < rows_ref[0, local], blended / sums, 0.0
        ).astype(jnp.bfloat16)


def text_kernel(q_ref, own_k, own_v, text_k, text_v, own_bias, text_bias, out_ref, level_ref):
    chunks = (
        (own_k[...], own_v[...], own_bias[...]),
        (text_k[...], text_v[...], text_bias[...]),
    )
    highest, sums, blended = softmax_blend(q_ref[...], chunks)
    out_ref[...] = (blended / sums).astype(jnp.bfloat16)
    level_ref[...] = jnp.broadcast_to(highest + jnp.log2(sums), level_ref.shape)


def column(rows):
    return pl.BlockSpec((rows, HD), lambda head, *_: (0, head))


def fixed(shape):
    return pl.BlockSpec(shape, lambda head, *_: (0,) * len(shape))


def shards(
    latent,
    text_tokens,
    mod_shift,
    mod_scale,
    mod_gate,
    project_in,
    project_out,
    q_gain,
    k_gain,
    pattern,
    tile_rows,
    text_mask,
):
    head_count = lax.axis_size("head")
    band_count = lax.axis_size("tile")
    band_index = lax.axis_index("tile")
    moved = lax.all_to_all(latent, "tile", split_axis=2, concat_axis=0, tiled=True)
    column_whole = lax.all_gather(moved, "head", axis=3, tiled=True)
    normed = modulate(column_whole, mod_shift, mod_scale).reshape(-1, D)
    own_q, own_k, own_v = prepare(normed, project_in, q_gain, k_gain)
    text_q, text_k, text_v = prepare(
        modulate(text_tokens, mod_shift, mod_scale), project_in, q_gain, k_gain
    )
    count, width = own_q.shape
    local_heads = width // HD
    per_device = F // TF * (H // TH)
    tile_size = TF * TH * TW
    slots = pattern.shape[1]
    forward = [(i, i + 1) for i in range(band_count - 1)]
    backward = [(target, source) for source, target in forward]
    low_k, low_v = (lax.ppermute(part, "tile", forward) for part in (own_k, own_v))
    high_k, high_v = (lax.ppermute(part, "tile", backward) for part in (own_k, own_v))

    positions = jnp.arange(tile_size, dtype=jnp.int32)
    text_usable = text_mask == 1
    slot_band = band_index + pattern // per_device - 1
    picked_rows = tile_rows[
        jnp.clip(slot_band, 0, band_count - 1) * per_device + pattern % per_device
    ]
    bias = jnp.where(positions < picked_rows[..., None], 0.0, MASKED).astype(jnp.float32)
    bias = bias.reshape(per_device, slots, 1, tile_size)
    text_bias = jnp.where(text_usable, 0.0, MASKED).astype(jnp.float32)[None]
    own_rows = lax.dynamic_slice_in_dim(tile_rows, band_index * per_device, per_device, 0)
    own_bias = jnp.where(positions[None] < own_rows[:, None], 0.0, MASKED)
    own_bias = own_bias.astype(jnp.float32).reshape(1, count)
    once_bias = jnp.where(band_index == 0, text_bias, MASKED)

    text_part, levels = pl.pallas_call(
        text_kernel,
        grid=(local_heads,),
        in_specs=[
            column(TEXT), column(count), column(count), column(TEXT), column(TEXT),
            fixed((1, count)), fixed((1, TEXT)),
        ],
        out_specs=[column(TEXT), column(TEXT)],
        out_shape=[
            jax.ShapeDtypeStruct((TEXT, width), jnp.bfloat16),
            jax.ShapeDtypeStruct((TEXT, width), jnp.float32),
        ],
        compiler_params=pltpu.CompilerParams(vmem_limit_bytes=48 << 20),
        cost_estimate=pl.CostEstimate(
            flops=4 * TEXT * (count + TEXT) * width, bytes_accessed=6 << 20, transcendentals=0
        ),
        name="text_attention",
    )(text_q, own_k, own_v, text_k, text_v, own_bias, once_bias)
    level = levels.reshape(TEXT, local_heads, HD)[:, :, 0]
    distance = 1
    while distance < band_count:
        pairs = [(i, i ^ distance) for i in range(band_count)]
        other_part = lax.ppermute(text_part, "tile", pairs)
        other_level = lax.ppermute(level, "tile", pairs)
        peak = jnp.maximum(level, other_level)
        mine, theirs = jnp.exp2(level - peak), jnp.exp2(other_level - peak)
        total = mine + theirs

        def widen(share):
            return jnp.repeat(share, HD, axis=1)

        text_part = (
            text_part.astype(jnp.float32) * widen(mine / total)
            + other_part.astype(jnp.float32) * widen(theirs / total)
        ).astype(jnp.bfloat16)
        level = peak + jnp.log2(total)
        distance *= 2

    filler = jnp.zeros((1, slots - per_device), jnp.int32)
    numbers = jnp.concatenate(
        [jnp.concatenate([own_rows[None].astype(jnp.int32), filler], 1), pattern], 0
    )
    latent_out = pl.pallas_call(
        functools.partial(latent_kernel, per_device, tile_size, slots),
        grid_spec=pltpu.PrefetchScalarGridSpec(
            num_scalar_prefetch=1,
            grid=(local_heads,),
            in_specs=[column(count)] * 7 + [column(TEXT)] * 2
            + [fixed((per_device, slots, 1, tile_size)), fixed((1, TEXT))],
            out_specs=column(count),
            scratch_shapes=[pltpu.VMEM((3 * per_device, tile_size, HD), jnp.bfloat16)] * 2,
        ),
        out_shape=jax.ShapeDtypeStruct((count, width), jnp.bfloat16),
        compiler_params=pltpu.CompilerParams(vmem_limit_bytes=48 << 20),
        cost_estimate=pl.CostEstimate(
            flops=4 * count * (slots * tile_size + TEXT) * width,
            bytes_accessed=10 << 20, transcendentals=0,
        ),
        name="latent_attention",
    )(numbers, own_q, own_k, own_v, low_k, low_v, high_k, high_v, text_k, text_v, bias, text_bias)

    latent_columns = latent_out.reshape(head_count, -1, width)
    text_blocks = text_part.reshape(head_count, -1, width)
    latent_share = latent_columns.shape[1]
    blocks = jnp.concatenate([latent_columns, text_blocks], 1)
    share = blocks.shape[1]
    bits = head_count.bit_length() - 1
    order = tuple(reversed(range(bits))) + (bits, bits + 1)
    joined = jnp.transpose(blocks.reshape((2,) * bits + (share, width)), order)
    joined = joined.reshape(2, -1, width)
    head_index = lax.axis_index("head")
    kept_total = None
    for step in range(bits):
        mine = (head_index >> step) & 1
        pairs = [(i, i ^ (1 << step)) for i in range(head_count)]
        if step == 0:

            def project(half):
                rows = lax.dynamic_index_in_dim(joined, half, 0, keepdims=False)
                term = jnp.dot(rows, project_out, preferred_element_type=jnp.float32)
                return term.astype(jnp.bfloat16)

            sent, kept = project(1 - mine), project(mine)
        else:
            halves = kept_total.reshape(2, -1, D)
            sent = lax.dynamic_index_in_dim(halves, 1 - mine, 0, keepdims=False)
            kept = lax.dynamic_index_in_dim(halves, mine, 0, keepdims=False)
            sent = sent.astype(jnp.bfloat16)
        arrived = lax.ppermute(sent, "head", pairs)
        kept_total = kept.astype(jnp.float32) + arrived.astype(jnp.float32)
    summed_rows = kept_total
    update = (
        (summed_rows[:latent_share] * mod_gate)
        .astype(jnp.bfloat16)
        .reshape(F // head_count, H, TW, D)
    )
    text_update = (summed_rows[latent_share:] * mod_gate).astype(jnp.bfloat16)
    return (update, text_update)


def solution(mesh):
    placed = (
        P(("group", "tile"), None, None, "head"),
        P("group", None),
        P(),
        P(),
        P(),
        P(None, None, "head"),
        P("head", None),
        P(),
        P(),
        P("tile", None),
        P("group"),
        P("group"),
    )
    return jax.shard_map(
        shards,
        mesh=mesh,
        in_specs=placed,
        out_specs=(P(("group", "head"), None, "tile", None), P(("group", "head"), None)),
        check_vma=False,
    )
```
